32 devices in a mesh: shard: 2 (over x), rep: 16 (over z, y, core).
Axes of the slice: x: 2, y: 2, z: 4, core: 2. Of those that a mesh axis runs over, the one named last changes fastest.
Arguments:
- tokens: bfloat16 [32768, 1024], P(('shard', 'rep')), may hold values from -6 to 6
- doc_lengths: int32 [32, 4], P(('shard', 'rep')), may hold values from 0 to 1024, as said below
- out_grad: bfloat16 [32768, 1024], P(('shard', 'rep')), may hold values from -6 to 6
- w_qkv: float32 [1024, 3072], P('shard'), may hold values from -0.25 to 0.25
- w_out: float32 [1024, 1024], P('shard'), may hold values from -0.5 to 0.5
- w_fc: float32 [1024, 4096], P('shard'), may hold values from -0.1875 to 0.1875
- w_proj: float32 [4096, 1024], P('shard'), may hold values from -0.09375 to 0.09375
- small_params: float32 [12288], P('shard')
- m_qkv: float32 [1024, 3072], P('shard'), may hold values from -128 to 128
- m_out: float32 [1024, 1024], P('shard'), may hold values from -64 to 64
- m_fc: float32 [1024, 4096], P('shard'), may hold values from -32 to 32
- m_proj: float32 [4096, 1024], P('shard'), may hold values from -64 to 64
- m_small: float32 [12288], P('shard'), may hold values from -128 to 128
- v_qkv: float32 [1024, 3072], P('shard'), may hold values from 32.768 to 131.072
- v_out: float32 [1024, 1024], P('shard'), may hold values from 8.192 to 32.768
- v_fc: float32 [1024, 4096], P('shard'), may hold values from 2.29376 to 9.17504
- v_proj: float32 [4096, 1024], P('shard'), may hold values from 8.192 to 32.768
- v_small: float32 [12288], P('shard'), may hold values from 32.768 to 131.072
Outputs:
- mixed: bfloat16 [32768, 1024], P(('shard', 'rep'))
- tokens_grad: float32 [32768, 1024], P(('shard', 'rep'))
- new_w_qkv: float32 [1024, 3072], P('shard')
- new_w_out: float32 [1024, 1024], P('shard')
- new_w_fc: float32 [1024, 4096], P('shard')
- new_w_proj: float32 [4096, 1024], P('shard')
- new_small: float32 [12288], P('shard')
- new_m_qkv: float32 [1024, 3072], P('shard')
- new_m_out: float32 [1024, 1024], P('shard')
- new_m_fc: float32 [1024, 4096], P('shard')
- new_m_proj: float32 [4096, 1024], P('shard')
- new_m_small: float32 [12288], P('shard')
- new_v_qkv: float32 [1024, 3072], P('shard')
- new_v_out: float32 [1024, 1024], P('shard')
- new_v_fc: float32 [1024, 4096], P('shard')
- new_v_proj: float32 [4096, 1024], P('shard')
- new_v_small: float32 [12288], P('shard')
The draws below stay inside these ranges and needn't reach their ends.
Inputs may be any that keep to these rules, and one draw needn't show every extreme that they name: `doc_lengths`: row r lists, in order, the lengths of the sequences packed from the start of device r's buffer (devices in the order of the tokens' rows); a row sums to at most 1024, the rest of the buffer is padding, and zero lengths are empty slots. In every draw one row holds a single sequence of 1024 tokens.
All inputs are finite; a program needn't handle non-finite values.
Results may differ from the reference program's by a relative error of at most 0.03.
Values may be sent and summed in bfloat16 or wider, within the bound.
A program may use at most 512 MiB of HBM per device.

```python
import math
import jax
import jax.numpy as jnp
from jax import lax

D = 1024
HEADS = 16
HD = 64
FF = 4096
CAP = 1024
SLOTS = 4
STEP = 10
NBUF = 32
TOKENS = 32768
SMALLP = 12288


def draw_doc_lengths(key, part):
    key = jax.random.fold_in(key, 11)
    key_load, key_full, key_cuts = jax.random.split(key, 3)
    buffer_loads = jax.random.randint(key_load, (NBUF, 1), CAP // 2, CAP + 1)
    chosen = jax.random.randint(key_full, (), 0, NBUF)
    cut_points = jax.random.randint(key_cuts, (NBUF, SLOTS - 1), 0, buffer_loads + 1)
    cut_points = jnp.sort(cut_points, axis=1)
    bounds = jnp.concatenate([jnp.zeros((NBUF, 1), jnp.int32), cut_points.astype(jnp.int32), buffer_loads.astype(jnp.int32)], axis=1)
    lengths = bounds[:, 1:] - bounds[:, :-1]
    single = jnp.zeros((SLOTS,), jnp.int32).at[0].set(CAP)
    row_ids = jnp.arange(NBUF)
    return jnp.where((row_ids == chosen)[:, None], single[None, :], lengths).astype(jnp.int32)


def draw_small_params(key, part):
    key = jax.random.fold_in(key, 23)
    key_gain, key_bias = jax.random.split(key)
    places = jnp.arange(8 * D + FF)
    is_gain = (places < D) | (places >= 5 * D) & (places < 6 * D)
    gain_draw = jax.random.uniform(key_gain, places.shape, jnp.float32, 0.7, 1.3)
    bias_draw = 0.2 * jax.random.normal(key_bias, places.shape, jnp.float32)
    return jnp.where(is_gain, gain_draw, bias_draw).astype(jnp.float32)


def level_of(stream_key, dims, cuts, least, high):
    def one(dim, blocks):
        heights = jax.random.uniform(jax.random.fold_in(jax.random.fold_in(stream_key, 6), dim), (blocks,), jnp.float32, least / len(cuts), high / len(cuts))
        return jnp.repeat(jnp.exp(heights), dims[dim] // blocks).reshape((-1,) + (1,) * (len(dims) - dim - 1))

    gain = one(*cuts[0])
    for cut in cuts[1:]:
        gain = gain * one(*cut)
    return gain


def centred(rng, shape, width, most, cuts=(), kind=jnp.bfloat16):
    values = jax.random.normal(rng, shape, jnp.float32) * width
    if len(cuts) > 0:
        values = level_of(rng, shape, cuts, -0.22, 0.18) * values
    return jnp.clip(values, min=-most, max=most).astype(kind)


def setup_inputs(seed: int = 0) -> dict:
    seeds = jax.random.split(jax.random.key(seed), 19)
    return {
        "tokens": centred(seeds[0], (TOKENS, D), 1.0, 6.0, ((0, 32),)),
        "doc_lengths": draw_doc_lengths(jax.random.fold_in(seeds[18], 71), 0),
        "out_grad": centred(seeds[2], (TOKENS, D), 1.0, 6.0, ((0, 32),)),
        "w_qkv": centred(seeds[3], (D, 3 * D), (D // 2) ** -0.5, 0.25, ((0, 2),), jnp.float32),
        "w_out": centred(seeds[4], (D, D), (D // 8) ** -0.5, 0.5, ((0, 2),), jnp.float32),
        "w_fc": centred(seeds[5], (D, FF), D ** -0.5, 0.1875, ((0, 2),), jnp.float32),
        "w_proj": centred(seeds[6], (FF, D), FF ** -0.5, 0.09375, ((0, 2),), jnp.float32),
        "small_params": draw_small_params(jax.random.fold_in(seeds[18], 71), 0),
        "m_qkv": centred(seeds[8], (D, 3 * D), (0.11 * TOKENS ** 0.5), 128.0, ((0, 2),), jnp.float32),
        "m_out": centred(seeds[9], (D, D), (0.055 * TOKENS ** 0.5), 64.0, ((0, 2),), jnp.float32),
        "m_fc": centred(seeds[10], (D, FF), (0.029 * TOKENS ** 0.5), 32.0, ((0, 2),), jnp.float32),
        "m_proj": centred(seeds[11], (FF, D), (0.055 * TOKENS ** 0.5), 64.0, ((0, 2),), jnp.float32),
        "m_small": centred(seeds[12], (SMALLP,), (0.11 * TOKENS ** 0.5), 128.0, ((0, 2),), jnp.float32),
        "v_qkv": jnp.clip(jnp.exp(math.log(131.072) - 1.3862944 * jax.random.uniform(seeds[13], (D, 3 * D), jnp.float32) ** level_of(seeds[13], (D, 3 * D), ((0, 2),), -0.2, 0.2)), 32.768, 131.072),
        "v_out": jnp.clip(jnp.exp(math.log(32.768) - 1.3862944 * jax.random.uniform(seeds[14], (D, D), jnp.float32) ** level_of(seeds[14], (D, D), ((0, 2),), -0.2, 0.2)), 8.192, 32.768),
        "v_fc": jnp.clip(jnp.exp(math.log(9.17504) - 1.3862944 * jax.random.uniform(seeds[15], (D, FF), jnp.float32) ** level_of(seeds[15], (D, FF), ((0, 2),), -0.2, 0.2)), 2.29376, 9.17504),
        "v_proj": jnp.clip(jnp.exp(math.log(32.768) - 1.3862944 * jax.random.uniform(seeds[16], (FF, D), jnp.float32) ** level_of(seeds[16], (FF, D), ((0, 2),), -0.2, 0.2)), 8.192, 32.768),
        "v_small": jnp.clip(jnp.exp(math.log(131.072) - 1.3862944 * jax.random.uniform(seeds[17], (SMALLP,), jnp.float32) ** level_of(seeds[17], (SMALLP,), ((0, 2),), -0.2, 0.2)), 32.768, 131.072),
    }


@jax.custom_vjp
def low(v):
    return lax.optimization_barrier(v.astype(jnp.bfloat16)).astype(jnp.float32)

@jax.custom_vjp
def low_back(v):
    return v

def low_keep(v):
    return (low(v), None)

def low_pass(kept, grad):
    return (grad,)

def back_keep(v):
    return (v, None)

def back_low(kept, grad):
    return (low(grad),)
low.defvjp(low_keep, low_pass)
low_back.defvjp(back_keep, back_low)
highest = lax.Precision.HIGHEST
beta_one = 0.9
beta_two = 0.999
eps_adam = 1e-08
norm_eps = 1e-05

def matmul(left, right):
    return jnp.dot(left, right, precision=highest, preferred_element_type=jnp.float32)

def layer_norm(values, gain_row, bias_row):
    average = lax.optimization_barrier(jnp.mean(values, axis=-1, keepdims=True))
    centered = values - average
    variance = lax.optimization_barrier(jnp.mean(centered * centered, axis=-1, keepdims=True))
    return centered * lax.rsqrt(variance + norm_eps) * gain_row + bias_row

def split_small(small):
    pieces = [small[number * D:(number + 1) * D] for number in range(8)]
    return pieces + [small[8 * D:]]

def buffer_masks(length_row):
    seq_ends = jnp.cumsum(length_row)
    places = jnp.arange(CAP, dtype=jnp.int32)
    segment = lax.optimization_barrier(jnp.sum((places[:, None] >= seq_ends[None, :]).astype(jnp.int32), axis=1))
    live = (places < seq_ends[-1]).astype(jnp.float32)
    allowed = (segment[:, None] == segment[None, :]) & (places[None, :] <= places[:, None])
    return (live, allowed)

def forward(tok_in, weight_qkv, weight_out, weight_fc, weight_proj, small, live, allowed):
    weight_qkv = low(weight_qkv)
    weight_out = low(weight_out)
    weight_fc = low(weight_fc)
    weight_proj = low(weight_proj)
    small = low(small)
    gain_one, bias_one, bias_q, bias_v, bias_o, gain_two, bias_two, bias_proj, bias_fc = split_small(small)
    normed = low(layer_norm(tok_in, gain_one, bias_one))
    qkv_bias = jnp.concatenate([bias_q, jnp.zeros_like(bias_q), bias_v])
    qkv_all = low_back(low(matmul(normed, weight_qkv) + qkv_bias))
    queries = qkv_all[:, :D].reshape(CAP, HEADS, HD)
    keys = qkv_all[:, D:2 * D].reshape(CAP, HEADS, HD)
    values = qkv_all[:, 2 * D:].reshape(CAP, HEADS, HD)
    scale = HD ** (-0.5)
    scores = jnp.einsum('qhd,khd->hqk', queries, keys, precision=highest) * scale
    scores = low_back(scores)
    masked = jnp.where(allowed[None], scores, -1e+30)
    weights_soft = jax.nn.softmax(masked, axis=-1)
    weights_low = low(weights_soft)
    attended = jnp.einsum('hqk,khd->qhd', weights_low, values, precision=highest).reshape(CAP, D)
    attended = low_back(low(attended))
    branch = low_back(matmul(attended, weight_out) + bias_o)
    middle = tok_in + branch
    normed_two = low(layer_norm(middle, gain_two, bias_two))
    hidden_pre = low_back(matmul(normed_two, weight_fc) + bias_fc)
    hidden_act = low(jax.nn.gelu(hidden_pre, approximate=True))
    result = low_back(matmul(hidden_act, weight_proj) + bias_proj)
    return (middle + result) * live[:, None]

def adamw(weight, first, second, grad, rate, decay):
    first_new = beta_one * first + (1.0 - beta_one) * grad
    second_new = beta_two * second + (1.0 - beta_two) * grad * grad
    first_hat = first_new / (1.0 - beta_one ** STEP)
    second_hat = second_new / (1.0 - beta_two ** STEP)
    weight_new = weight - rate * (first_hat / (jnp.sqrt(second_hat) + eps_adam) + decay * weight)
    return (weight_new, first_new, second_new)

def reference(tokens, doc_lengths, out_grad, w_qkv, w_out, w_fc, w_proj, small_params, m_qkv, m_out, m_fc, m_proj, m_small, v_qkv, v_out, v_fc, v_proj, v_small):
    tok_blocks = tokens.astype(jnp.float32).reshape(NBUF, CAP, D)
    cot_blocks = out_grad.astype(jnp.float32).reshape(NBUF, CAP, D)

    def one_buffer(totals, inputs):
        tok_rows, cot_rows, length_row = inputs
        live, allowed = buffer_masks(length_row)

        def wrapped(tok_in, weight_qkv, weight_out, weight_fc, weight_proj, small):
            return forward(tok_in, weight_qkv, weight_out, weight_fc, weight_proj, small, live, allowed)
        outputs, pullback = jax.vjp(wrapped, tok_rows, w_qkv, w_out, w_fc, w_proj, small_params)
        cotangents = pullback(cot_rows)
        new_totals = tuple((total_now + grad_now for total_now, grad_now in zip(totals, cotangents[1:])))
        return (new_totals, (outputs.astype(jnp.bfloat16), cotangents[0]))
    zero_totals = (jnp.zeros_like(w_qkv), jnp.zeros_like(w_out), jnp.zeros_like(w_fc), jnp.zeros_like(w_proj), jnp.zeros_like(small_params))
    grads, stacked = lax.scan(one_buffer, zero_totals, (tok_blocks, cot_blocks, doc_lengths))
    out_blocks, grad_blocks = stacked
    mixed = out_blocks.reshape(TOKENS, D)
    tokens_grad = grad_blocks.reshape(TOKENS, D)
    grad_qkv, grad_out, grad_fc, grad_proj, grad_small = grads
    new_w_qkv, new_m_qkv, new_v_qkv = adamw(w_qkv, m_qkv, v_qkv, grad_qkv, 0.05, 0.1)
    new_w_out, new_m_out, new_v_out = adamw(w_out, m_out, v_out, grad_out, 0.05, 0.1)
    new_w_fc, new_m_fc, new_v_fc = adamw(w_fc, m_fc, v_fc, grad_fc, 0.05, 0.1)
    new_w_proj, new_m_proj, new_v_proj = adamw(w_proj, m_proj, v_proj, grad_proj, 0.05, 0.1)
    new_small, new_m_small, new_v_small = adamw(small_params, m_small, v_small, grad_small, 0.5, 0.0)
    return (mixed, tokens_grad, new_w_qkv, new_w_out, new_w_fc, new_w_proj, new_small, new_m_qkv, new_m_out, new_m_fc, new_m_proj, new_m_small, new_v_qkv, new_v_out, new_v_fc, new_v_proj, new_v_small)
```

```python
import jax
import jax.numpy as jnp
from jax import lax
from jax.sharding import PartitionSpec as P

D = 1024
HEADS = 16
HD = 64
STEP = 10


beta_one = 0.9
beta_two = 0.999
eps_adam = 1e-08
norm_eps = 1e-05


def layer_norm(values, gain_row, bias_row):
    average = jnp.mean(values, axis=-1, keepdims=True)
    centered = values - average
    variance = jnp.mean(centered * centered, axis=-1, keepdims=True)
    return centered * lax.rsqrt(variance + norm_eps) * gain_row + bias_row


def gelu_tanh(values):
    return jax.nn.gelu(values, approximate=True)


def contract_rows(left, right):
    return lax.dot_general(
        left, right, (((0,), (0,)), ((), ())), preferred_element_type=jnp.float32
    )


def contract_cols(left, right):
    return lax.dot_general(
        left, right, (((1,), (1,)), ((), ())), preferred_element_type=jnp.float32
    )


def split_small(small):
    pieces = [small[number * D : (number + 1) * D] for number in range(8)]
    return pieces + [small[8 * D :]]


def adamw(weight, first, second, grad, rate, decay):
    first_new = beta_one * first + (1.0 - beta_one) * grad
    second_new = beta_two * second + (1.0 - beta_two) * grad * grad
    first_hat = first_new / (1.0 - beta_one**STEP)
    second_hat = second_new / (1.0 - beta_two**STEP)
    weight_new = weight - rate * (first_hat / (jnp.sqrt(second_hat) + eps_adam) + decay * weight)
    return (weight_new, first_new, second_new)


def block_mask(segment, first_row, block_rows):
    places = jnp.arange(segment.shape[0], dtype=jnp.int32)
    query_seg = segment[first_row : first_row + block_rows]
    query_pos = places[first_row : first_row + block_rows]
    return (query_seg[:, None] == segment[None, :]) & (places[None, :] <= query_pos[:, None])


def block_scores(q_block, keys, allowed, scale):
    scores = jnp.einsum("qhd,khd->hqk", q_block, keys, preferred_element_type=jnp.float32) * scale
    return jnp.where(allowed[None], scores, -1e30)


def attend_forward(queries, keys, values, segment, scale):
    row_count = queries.shape[0]
    block_rows = min(256, row_count)
    outputs = []
    weights = []
    for first_row in range(0, row_count, block_rows):
        last_row = first_row + block_rows
        allowed = block_mask(segment, first_row, block_rows)[:, :last_row]
        masked = block_scores(queries[first_row:last_row], keys[:last_row], allowed, scale)
        top_score = jnp.max(masked, axis=-1, keepdims=True)
        expo_vals = jnp.exp(masked - top_score)
        totals = jnp.sum(expo_vals, axis=-1, keepdims=True)
        weights_low = (expo_vals / totals).astype(jnp.bfloat16)
        outputs.append(
            jnp.einsum(
                "hqk,khd->qhd", weights_low, values[:last_row], preferred_element_type=jnp.float32
            )
        )
        weights.append(weights_low)
    return (outputs, weights)


def attend_backward(queries, keys, values, outputs, weights, d_att, scale):
    row_count = queries.shape[0]
    block_rows = row_count // len(weights)
    d_queries = []
    d_keys = jnp.zeros(keys.shape, jnp.float32)
    d_values = jnp.zeros(values.shape, jnp.float32)
    for number, weights_low in enumerate(weights):
        first_row = number * block_rows
        last_row = first_row + block_rows
        q_block = queries[first_row:last_row]
        g_block = d_att[first_row:last_row]
        d_probs = jnp.einsum(
            "qhd,khd->hqk", g_block, values[:last_row], preferred_element_type=jnp.float32
        )
        inner = jnp.sum(outputs[number] * g_block.astype(jnp.float32), axis=-1).T[:, :, None]
        d_scores = (weights_low.astype(jnp.float32) * (d_probs - inner)).astype(jnp.bfloat16)
        d_queries.append(
            jnp.einsum("hqk,khd->qhd", d_scores, keys[:last_row], preferred_element_type=jnp.float32)
            * scale
        )
        below = ((0, row_count - last_row), (0, 0), (0, 0))
        d_keys = d_keys + jnp.pad(
            jnp.einsum("hqk,qhd->khd", d_scores, q_block, preferred_element_type=jnp.float32)
            * scale,
            below,
        )
        d_values = d_values + jnp.pad(
            jnp.einsum("hqk,qhd->khd", weights_low, g_block, preferred_element_type=jnp.float32),
            below,
        )
    return (jnp.concatenate(d_queries, axis=0), d_keys, d_values)


def gather_weight(weight):
    rows = weight.shape[0] // lax.axis_size("rep")
    part = lax.dynamic_slice_in_dim(weight, lax.axis_index("rep") * rows, rows, axis=0)
    return lax.all_gather(part.astype(jnp.bfloat16), ("shard", "rep"), axis=0, tiled=True)


def reduce_grad(grad):
    part = lax.psum_scatter(
        grad.astype(jnp.bfloat16), ("shard", "rep"), scatter_dimension=0, tiled=True
    )
    return lax.all_gather(part, "rep", axis=0, tiled=True).astype(jnp.float32)


def per_device(
    tokens,
    doc_lengths,
    out_grad,
    w_qkv,
    w_out,
    w_fc,
    w_proj,
    small_params,
    m_qkv,
    m_out,
    m_fc,
    m_proj,
    m_small,
    v_qkv,
    v_out,
    v_fc,
    v_proj,
    v_small,
):
    row_count = tokens.shape[0]
    scale = HD ** (-0.5)
    seq_ends = jnp.cumsum(doc_lengths[0])
    places = jnp.arange(row_count, dtype=jnp.int32)
    segment = jnp.sum((places[:, None] >= seq_ends[None, :]).astype(jnp.int32), axis=1)
    live = (places < seq_ends[-1]).astype(jnp.float32)[:, None]
    qkv_full, out_full, small_full = (
        gather_weight(w_qkv),
        gather_weight(w_out),
        lax.all_gather(small_params.astype(jnp.bfloat16), "shard", axis=0, tiled=True),
    )
    gain_one, bias_one, bias_q, bias_v, bias_o, gain_two, bias_two, bias_proj, bias_fc = (
        split_small(small_full.astype(jnp.float32))
    )
    tok_float = tokens.astype(jnp.float32)
    normed_one, norm_one_back = jax.vjp(layer_norm, tok_float, gain_one, bias_one)
    normed_low = normed_one.astype(jnp.bfloat16)
    qkv_bias = jnp.concatenate([bias_q, jnp.zeros_like(bias_q), bias_v])
    qkv_low = (jnp.dot(normed_low, qkv_full, preferred_element_type=jnp.float32) + qkv_bias).astype(
        jnp.bfloat16
    )
    queries = qkv_low[:, :D].reshape(row_count, HEADS, HD)
    keys = qkv_low[:, D : 2 * D].reshape(row_count, HEADS, HD)
    values = qkv_low[:, 2 * D :].reshape(row_count, HEADS, HD)
    outputs, weights = attend_forward(queries, keys, values, segment, scale)
    attended_low = jnp.concatenate(outputs, axis=0).reshape(row_count, D).astype(jnp.bfloat16)
    middle = (
        tok_float + jnp.dot(attended_low, out_full, preferred_element_type=jnp.float32) + bias_o
    )
    fc_full, proj_full = (
        gather_weight(w_fc),
        gather_weight(w_proj),
    )
    normed_two, norm_two_back = jax.vjp(layer_norm, middle, gain_two, bias_two)
    normed_two_low = normed_two.astype(jnp.bfloat16)
    hidden_pre = jnp.dot(normed_two_low, fc_full, preferred_element_type=jnp.float32) + bias_fc
    hidden_act, gelu_back = jax.vjp(gelu_tanh, hidden_pre)
    hidden_low = hidden_act.astype(jnp.bfloat16)
    result = jnp.dot(hidden_low, proj_full, preferred_element_type=jnp.float32) + bias_proj
    mixed = ((middle + result) * live).astype(jnp.bfloat16)
    d_out_f = out_grad.astype(jnp.float32) * live
    d_out_low = d_out_f.astype(jnp.bfloat16)
    grad_proj = contract_rows(hidden_low, d_out_low)
    grad_bias_proj = jnp.sum(d_out_low.astype(jnp.float32), axis=0)
    d_hidden = contract_cols(d_out_low, proj_full)
    d_pre_low = gelu_back(d_hidden)[0].astype(jnp.bfloat16)
    grad_fc = contract_rows(normed_two_low, d_pre_low)
    grad_bias_fc = jnp.sum(d_pre_low.astype(jnp.float32), axis=0)
    d_normed_two = contract_cols(d_pre_low, fc_full)
    d_mid_norm, grad_gain_two, grad_bias_two = norm_two_back(d_normed_two)
    d_middle = d_out_f + d_mid_norm
    d_branch = d_middle.astype(jnp.bfloat16)
    grad_out = contract_rows(attended_low, d_branch)
    grad_bias_o = jnp.sum(d_branch.astype(jnp.float32), axis=0)
    d_att = contract_cols(d_branch, out_full).astype(jnp.bfloat16).reshape(row_count, HEADS, HD)
    d_queries, d_keys, d_values = attend_backward(
        queries, keys, values, outputs, weights, d_att, scale
    )
    d_qkv = jnp.concatenate(
        [
            d_queries.reshape(row_count, D),
            d_keys.reshape(row_count, D),
            d_values.reshape(row_count, D),
        ],
        axis=1,
    ).astype(jnp.bfloat16)
    grad_qkv = contract_rows(normed_low, d_qkv)
    d_qkv_float = d_qkv.astype(jnp.float32)
    grad_bias_q = jnp.sum(d_qkv_float[:, :D], axis=0)
    grad_bias_v = jnp.sum(d_qkv_float[:, 2 * D :], axis=0)
    d_normed = contract_cols(d_qkv, qkv_full)
    d_tok_norm, grad_gain_one, grad_bias_one = norm_one_back(d_normed)
    tokens_grad = d_middle + d_tok_norm
    grad_small = jnp.concatenate(
        [
            grad_gain_one,
            grad_bias_one,
            grad_bias_q,
            grad_bias_v,
            grad_bias_o,
            grad_gain_two,
            grad_bias_two,
            grad_bias_proj,
            grad_bias_fc,
        ]
    )
    summed_proj = reduce_grad(grad_proj)
    summed_fc = reduce_grad(grad_fc)
    summed_out = reduce_grad(grad_out)
    summed_qkv = reduce_grad(grad_qkv)
    small_rows = small_params.shape[0]
    summed_small = lax.dynamic_slice_in_dim(
        lax.psum(grad_small, ("shard", "rep")), lax.axis_index("shard") * small_rows, small_rows
    )
    new_w_qkv, new_m_qkv, new_v_qkv = adamw(w_qkv, m_qkv, v_qkv, summed_qkv, 0.05, 0.1)
    new_w_out, new_m_out, new_v_out = adamw(w_out, m_out, v_out, summed_out, 0.05, 0.1)
    new_w_fc, new_m_fc, new_v_fc = adamw(w_fc, m_fc, v_fc, summed_fc, 0.05, 0.1)
    new_w_proj, new_m_proj, new_v_proj = adamw(w_proj, m_proj, v_proj, summed_proj, 0.05, 0.1)
    new_small, new_m_small, new_v_small = adamw(
        small_params, m_small, v_small, summed_small, 0.5, 0.0
    )
    return (
        mixed,
        tokens_grad,
        new_w_qkv,
        new_w_out,
        new_w_fc,
        new_w_proj,
        new_small,
        new_m_qkv,
        new_m_out,
        new_m_fc,
        new_m_proj,
        new_m_small,
        new_v_qkv,
        new_v_out,
        new_v_fc,
        new_v_proj,
        new_v_small,
    )


def solution(mesh):
    return jax.shard_map(
        per_device,
        mesh=mesh,
        in_specs=(
            P(("shard", "rep"), None),
            P(("shard", "rep"), None),
            P(("shard", "rep"), None),
            P("shard", None),
            P("shard", None),
            P("shard", None),
            P("shard", None),
            P("shard"),
            P("shard", None),
            P("shard", None),
            P("shard", None),
            P("shard", None),
            P("shard"),
            P("shard", None),
            P("shard", None),
            P("shard", None),
            P("shard", None),
            P("shard"),
        ),
        out_specs=(
            P(("shard", "rep"), None),
            P(("shard", "rep"), None),
            P("shard", None),
            P("shard", None),
            P("shard", None),
            P("shard", None),
            P("shard"),
            P("shard", None),
            P("shard", None),
            P("shard", None),
            P("shard", None),
            P("shard"),
            P("shard", None),
            P("shard", None),
            P("shard", None),
            P("shard", None),
            P("shard"),
        ),
        check_vma=False,
    )
```

```python
import jax
import jax.numpy as jnp
from jax import lax
from jax.sharding import PartitionSpec as P

D = 1024
HEADS = 16
HD = 64
STEP = 10


beta_one = 0.9
beta_two = 0.999
eps_adam = 1e-08
norm_eps = 1e-05


def layer_norm(values, gain_row, bias_row):
    average = jnp.mean(values, axis=-1, keepdims=True)
    centered = values - average
    variance = jnp.mean(centered * centered, axis=-1, keepdims=True)
    return centered * lax.rsqrt(variance + norm_eps) * gain_row + bias_row


def gelu_tanh(values):
    return jax.nn.gelu(values, approximate=True)


def contract_rows(left, right):
    return lax.dot_general(
        left, right, (((0,), (0,)), ((), ())), preferred_element_type=jnp.float32
    )


def contract_cols(left, right):
    return lax.dot_general(
        left, right, (((1,), (1,)), ((), ())), preferred_element_type=jnp.float32
    )


def split_small(small):
    pieces = [small[number * D : (number + 1) * D] for number in range(8)]
    return pieces + [small[8 * D :]]


def adamw(weight, first, second, grad, rate, decay):
    first_new = beta_one * first + (1.0 - beta_one) * grad
    second_new = beta_two * second + (1.0 - beta_two) * grad * grad
    first_hat = first_new / (1.0 - beta_one**STEP)
    second_hat = second_new / (1.0 - beta_two**STEP)
    weight_new = weight - rate * (first_hat / (jnp.sqrt(second_hat) + eps_adam) + decay * weight)
    return (weight_new, first_new, second_new)


def block_mask(segment, first_row, block_rows):
    places = jnp.arange(segment.shape[0], dtype=jnp.int32)
    query_seg = segment[first_row : first_row + block_rows]
    query_pos = places[first_row : first_row + block_rows]
    return (query_seg[:, None] == segment[None, :]) & (places[None, :] <= query_pos[:, None])


def block_scores(q_block, keys, allowed, scale):
    scores = jnp.einsum("qhd,khd->hqk", q_block, keys, preferred_element_type=jnp.float32) * scale
    return jnp.where(allowed[None], scores, -1e30)


def attend_forward(queries, keys, values, segment, scale):
    row_count = queries.shape[0]
    block_rows = min(256, row_count)
    outputs = []
    weights = []
    for first_row in range(0, row_count, block_rows):
        last_row = first_row + block_rows
        allowed = block_mask(segment, first_row, block_rows)[:, :last_row]
        masked = block_scores(queries[first_row:last_row], keys[:last_row], allowed, scale)
        top_score = jnp.max(masked, axis=-1, keepdims=True)
        expo_vals = jnp.exp(masked - top_score)
        totals = jnp.sum(expo_vals, axis=-1, keepdims=True)
        weights_low = (expo_vals / totals).astype(jnp.bfloat16)
        outputs.append(
            jnp.einsum(
                "hqk,khd->qhd", weights_low, values[:last_row], preferred_element_type=jnp.float32
            )
        )
        weights.append(weights_low)
    return (outputs, weights)


def attend_backward(queries, keys, values, outputs, weights, d_att, scale):
    row_count = queries.shape[0]
    block_rows = row_count // len(weights)
    d_queries = []
    d_keys = jnp.zeros(keys.shape, jnp.float32)
    d_values = jnp.zeros(values.shape, jnp.float32)
    for number, weights_low in enumerate(weights):
        first_row = number * block_rows
        last_row = first_row + block_rows
        q_block = queries[first_row:last_row]
        g_block = d_att[first_row:last_row]
        d_probs = jnp.einsum(
            "qhd,khd->hqk", g_block, values[:last_row], preferred_element_type=jnp.float32
        )
        inner = jnp.sum(outputs[number] * g_block.astype(jnp.float32), axis=-1).T[:, :, None]
        d_scores = (weights_low.astype(jnp.float32) * (d_probs - inner)).astype(jnp.bfloat16)
        d_queries.append(
            jnp.einsum("hqk,khd->qhd", d_scores, keys[:last_row], preferred_element_type=jnp.float32)
            * scale
        )
        below = ((0, row_count - last_row), (0, 0), (0, 0))
        d_keys = d_keys + jnp.pad(
            jnp.einsum("hqk,qhd->khd", d_scores, q_block, preferred_element_type=jnp.float32)
            * scale,
            below,
        )
        d_values = d_values + jnp.pad(
            jnp.einsum("hqk,qhd->khd", weights_low, g_block, preferred_element_type=jnp.float32),
            below,
        )
    return (jnp.concatenate(d_queries, axis=0), d_keys, d_values)


def gather_weight(weight):
    rows = weight.shape[0] // lax.axis_size("rep")
    part = lax.dynamic_slice_in_dim(weight, lax.axis_index("rep") * rows, rows, axis=0)
    return lax.all_gather(part.astype(jnp.bfloat16), ("shard", "rep"), axis=0, tiled=True)


def own_rows(total, rows):
    return lax.dynamic_slice_in_dim(
        total, lax.axis_index("shard") * rows, rows, axis=0
    ).astype(jnp.float32)


def per_device(
    tokens,
    doc_lengths,
    out_grad,
    w_qkv,
    w_out,
    w_fc,
    w_proj,
    small_params,
    m_qkv,
    m_out,
    m_fc,
    m_proj,
    m_small,
    v_qkv,
    v_out,
    v_fc,
    v_proj,
    v_small,
):
    row_count = tokens.shape[0]
    scale = HD ** (-0.5)
    seq_ends = jnp.cumsum(doc_lengths[0])
    places = jnp.arange(row_count, dtype=jnp.int32)
    segment = jnp.sum((places[:, None] >= seq_ends[None, :]).astype(jnp.int32), axis=1)
    live = (places < seq_ends[-1]).astype(jnp.float32)[:, None]
    qkv_full, out_full, small_full = (
        gather_weight(w_qkv),
        gather_weight(w_out),
        lax.all_gather(small_params.astype(jnp.bfloat16), "shard", axis=0, tiled=True),
    )
    gain_one, bias_one, bias_q, bias_v, bias_o, gain_two, bias_two, bias_proj, bias_fc = (
        split_small(small_full.astype(jnp.float32))
    )
    tok_float = tokens.astype(jnp.float32)
    normed_one, norm_one_back = jax.vjp(layer_norm, tok_float, gain_one, bias_one)
    normed_low = normed_one.astype(jnp.bfloat16)
    qkv_bias = jnp.concatenate([bias_q, jnp.zeros_like(bias_q), bias_v])
    qkv_low = (jnp.dot(normed_low, qkv_full, preferred_element_type=jnp.float32) + qkv_bias).astype(
        jnp.bfloat16
    )
    queries = qkv_low[:, :D].reshape(row_count, HEADS, HD)
    keys = qkv_low[:, D : 2 * D].reshape(row_count, HEADS, HD)
    values = qkv_low[:, 2 * D :].reshape(row_count, HEADS, HD)
    outputs, weights = attend_forward(queries, keys, values, segment, scale)
    attended_low = jnp.concatenate(outputs, axis=0).reshape(row_count, D).astype(jnp.bfloat16)
    middle = (
        tok_float + jnp.dot(attended_low, out_full, preferred_element_type=jnp.float32) + bias_o
    )
    fc_full, proj_full = (
        gather_weight(w_fc),
        gather_weight(w_proj),
    )
    normed_two, norm_two_back = jax.vjp(layer_norm, middle, gain_two, bias_two)
    normed_two_low = normed_two.astype(jnp.bfloat16)
    hidden_pre = jnp.dot(normed_two_low, fc_full, preferred_element_type=jnp.float32) + bias_fc
    hidden_act, gelu_back = jax.vjp(gelu_tanh, hidden_pre)
    hidden_low = hidden_act.astype(jnp.bfloat16)
    result = jnp.dot(hidden_low, proj_full, preferred_element_type=jnp.float32) + bias_proj
    mixed = ((middle + result) * live).astype(jnp.bfloat16)
    d_out_f = out_grad.astype(jnp.float32) * live
    d_out_low = d_out_f.astype(jnp.bfloat16)
    grad_proj = contract_rows(hidden_low, d_out_low)
    grad_bias_proj = jnp.sum(d_out_low.astype(jnp.float32), axis=0)
    d_hidden = contract_cols(d_out_low, proj_full)
    d_pre_low = gelu_back(d_hidden)[0].astype(jnp.bfloat16)
    grad_fc = contract_rows(normed_two_low, d_pre_low)
    grad_bias_fc = jnp.sum(d_pre_low.astype(jnp.float32), axis=0)
    d_normed_two = contract_cols(d_pre_low, fc_full)
    d_mid_norm, grad_gain_two, grad_bias_two = norm_two_back(d_normed_two)
    d_middle = d_out_f + d_mid_norm
    d_branch = d_middle.astype(jnp.bfloat16)
    d_branch, proj_low, fc_low = lax.optimization_barrier(
        (d_branch, grad_proj.astype(jnp.bfloat16), grad_fc.astype(jnp.bfloat16))
    )
    grad_out = contract_rows(attended_low, d_branch)
    grad_bias_o = jnp.sum(d_branch.astype(jnp.float32), axis=0)
    d_att = contract_cols(d_branch, out_full).astype(jnp.bfloat16).reshape(row_count, HEADS, HD)
    d_queries, d_keys, d_values = attend_backward(
        queries, keys, values, outputs, weights, d_att, scale
    )
    d_qkv = jnp.concatenate(
        [
            d_queries.reshape(row_count, D),
            d_keys.reshape(row_count, D),
            d_values.reshape(row_count, D),
        ],
        axis=1,
    ).astype(jnp.bfloat16)
    grad_qkv = contract_rows(normed_low, d_qkv)
    d_qkv_float = d_qkv.astype(jnp.float32)
    grad_bias_q = jnp.sum(d_qkv_float[:, :D], axis=0)
    grad_bias_v = jnp.sum(d_qkv_float[:, 2 * D :], axis=0)
    d_normed = contract_cols(d_qkv, qkv_full)
    d_tok_norm, grad_gain_one, grad_bias_one = norm_one_back(d_normed)
    tokens_grad = d_middle + d_tok_norm
    grad_small = jnp.concatenate(
        [
            grad_gain_one,
            grad_bias_one,
            grad_bias_q,
            grad_bias_v,
            grad_bias_o,
            grad_gain_two,
            grad_bias_two,
            grad_bias_proj,
            grad_bias_fc,
        ]
    )
    everywhere = ("shard", "rep")
    total_proj = lax.psum(proj_low, everywhere)
    total_proj, fc_low = lax.optimization_barrier((total_proj, fc_low))
    total_fc = lax.psum(fc_low, everywhere)
    total_fc, qkv_grad_low, out_grad_low = lax.optimization_barrier(
        (total_fc, grad_qkv.astype(jnp.bfloat16), grad_out.astype(jnp.bfloat16))
    )
    total_qkv, total_out = lax.psum((qkv_grad_low, out_grad_low), everywhere)
    total_small = lax.psum(grad_small, everywhere)
    summed_proj = own_rows(total_proj, w_proj.shape[0])
    summed_fc = own_rows(total_fc, w_fc.shape[0])
    summed_out = own_rows(total_out, w_out.shape[0])
    summed_qkv = own_rows(total_qkv, w_qkv.shape[0])
    summed_small = own_rows(total_small, small_params.shape[0])
    new_w_qkv, new_m_qkv, new_v_qkv = adamw(w_qkv, m_qkv, v_qkv, summed_qkv, 0.05, 0.1)
    new_w_out, new_m_out, new_v_out = adamw(w_out, m_out, v_out, summed_out, 0.05, 0.1)
    new_w_fc, new_m_fc, new_v_fc = adamw(w_fc, m_fc, v_fc, summed_fc, 0.05, 0.1)
    new_w_proj, new_m_proj, new_v_proj = adamw(w_proj, m_proj, v_proj, summed_proj, 0.05, 0.1)
    new_small, new_m_small, new_v_small = adamw(
        small_params, m_small, v_small, summed_small, 0.5, 0.0
    )
    return (
        mixed,
        tokens_grad,
        new_w_qkv,
        new_w_out,
        new_w_fc,
        new_w_proj,
        new_small,
        new_m_qkv,
        new_m_out,
        new_m_fc,
        new_m_proj,
        new_m_small,
        new_v_qkv,
        new_v_out,
        new_v_fc,
        new_v_proj,
        new_v_small,
    )


def solution(mesh):
    return jax.shard_map(
        per_device,
        mesh=mesh,
        in_specs=(
            P(("shard", "rep"), None),
            P(("shard", "rep"), None),
            P(("shard", "rep"), None),
            P("shard", None),
            P("shard", None),
            P("shard", None),
            P("shard", None),
            P("shard"),
            P("shard", None),
            P("shard", None),
            P("shard", None),
            P("shard", None),
            P("shard"),
            P("shard", None),
            P("shard", None),
            P("shard", None),
            P("shard", None),
            P("shard"),
        ),
        out_specs=(
            P(("shard", "rep"), None),
            P(("shard", "rep"), None),
            P("shard", None),
            P("shard", None),
            P("shard", None),
            P("shard", None),
            P("shard"),
            P("shard", None),
            P("shard", None),
            P("shard", None),
            P("shard", None),
            P("shard"),
            P("shard", None),
            P("shard", None),
            P("shard", None),
            P("shard", None),
            P("shard"),
        ),
        check_vma=False,
    )
```
